32 devices in a mesh: groups: 2 (over y), tm: 4 (over z), dp: 2 (over x), head: 2 (over core).
Axes of the slice: x: 2, y: 2, z: 4, core: 2. Of those that a mesh axis runs over, the one named last changes fastest.
Arguments:
- tokens: bfloat16 [4, 8, 256, 1024], P(('groups', 'dp'), 'tm'), parts along dimension 0, may hold values from -6 to 6
- counts: int32 [4, 8], P(('groups', 'dp'), 'tm'), parts along dimension 0, may hold values from 64 to 256, as said below
- positions: int32 [4, 8, 256], P(('groups', 'dp'), 'tm'), parts along dimension 0, may hold values from 0 to 255, as said below
- cotangent: bfloat16 [4, 8, 256, 1024], P(('groups', 'dp'), 'tm'), parts along dimension 0, may hold values from -6 to 6
- w_qkv: bfloat16 [3, 1024, 1024], P(None, 'dp', 'head'), may hold values from -8 to 8
- w_out: bfloat16 [1024, 1024], P('head', 'dp'), may hold values from -0.1875 to 0.1875
Outputs:
- block_out: bfloat16 [4, 8, 256, 1024], P(('groups', 'dp'), 'tm'), parts along dimension 0
- token_grad: bfloat16 [4, 8, 256, 1024], P(('groups', 'dp'), 'tm'), parts along dimension 0
- out_weight_grad: float32 [2048, 1024], P(('groups', 'head'), 'dp'), parts along dimension 0
The draws below stay inside these ranges and needn't reach their ends.
There are 2 independent parts, one for each index of `groups`. The reference program is written for one: setup_inputs(seed, part) draws one part's arguments, and reference() takes and returns one part's arrays. A program takes and returns all parts, laid end to end along the dimension named above; an argument that names none is the same for every part. Nothing has to cross between parts.
Inputs may be any that keep to these rules, and one draw needn't show every extreme that they name: `counts`: frame 0 of every clip keeps all 256 positions; every other frame keeps between 64 and 192. Each frame's row is a permutation of 0 to 255: the kept positions in ascending order in the first counts slots, then the others in ascending order.
All inputs are finite; a program needn't handle non-finite values.
Results may differ from the reference program's by a relative error of at most 0.012.
The reference program's roundings to bfloat16 on the way count: a program that leaves them out, or rounds other values in their place, can miss the bound.
Values may be sent and summed in bfloat16 or wider, within the bound.
A program may use at most 64 MiB of HBM per device.

```python
import jax
import jax.numpy as jnp
from jax import lax

D = 1024
HD = 64
P_SIZE = 256
FRAMES = 8
CLIPS = 2
N_HEAD = 2


def draw_layout(key):
    frame_ids = jnp.arange(FRAMES, dtype=jnp.int32)
    kept_counts = jax.random.randint(jax.random.fold_in(key, 101), (CLIPS, FRAMES), P_SIZE // 4, 3 * P_SIZE // 4 + 1, dtype=jnp.int32)
    kept_counts = jnp.where(frame_ids[None, :] == 0, P_SIZE, kept_counts).astype(jnp.int32)
    slot_ids = jnp.arange(P_SIZE, dtype=jnp.int32)
    ranking = jax.random.randint(jax.random.fold_in(key, 102), (CLIPS, FRAMES, P_SIZE), 0, 1 << 20, dtype=jnp.int32) * P_SIZE + slot_ids
    order = jnp.argsort(ranking, axis=-1)
    standing = jnp.argsort(order, axis=-1)
    kept_flag = standing < kept_counts[:, :, None]
    layout = jnp.argsort(jnp.where(kept_flag, 0, P_SIZE) + slot_ids, axis=-1).astype(jnp.int32)
    return (kept_counts, layout)


def draw_counts(key, part):
    shared = draw_layout(key)
    return shared[0]


def draw_positions(key, part):
    shared = draw_layout(key)
    return shared[1]


def draw_tokens(key, part):
    key = jax.random.fold_in(key, 7)
    shape = (CLIPS, FRAMES, P_SIZE, D)
    values = jax.random.normal(key, shape, jnp.float32)
    return jnp.clip(values, -6.0, 6.0).astype(jnp.bfloat16)


def draw_w_qkv(key, part):
    key = jax.random.fold_in(key, 5)
    base = jnp.clip(jax.random.normal(key, (3, D, D), jnp.float32), -6.0, 6.0) * D ** (-0.5)
    return jnp.clip(base, -8.0, 8.0).astype(jnp.bfloat16)


def spiked(array, key, source, target, parts, factor):
    def block_of(dim):
        return (jnp.arange(array.shape[dim]) // (array.shape[dim] // parts)).reshape((-1,) + (1,) * (array.ndim - 1 - dim))

    first = jax.random.permutation(key, parts)[block_of(target)]
    second = (block_of(target) + parts // 2) % parts
    return jnp.where((block_of(source) == first) | (block_of(source) == second), factor * array, array)


def block_levels(key, extent, split, smallest, largest):
    loudness, own = 1.0, jax.random.fold_in(key, 6)
    for position, parts in split:
        heights = jnp.exp(jax.random.uniform(jax.random.fold_in(own, position), (parts,), jnp.float32, smallest / len(split), largest / len(split)))
        loudness = loudness * jnp.repeat(heights, extent[position] // parts).reshape([-1 if axis == position else 1 for axis in range(len(extent))])
    return loudness


def noise(own_key, dims, deviation, reach, split=(), kind=jnp.bfloat16):
    values = jax.random.normal(own_key, dims, jnp.float32) * deviation
    if len(split) > 0:
        values = block_levels(own_key, dims, split, -0.22, 0.18) * values
    return jnp.clip(values, min=-reach, max=reach).astype(kind)


def heavy_noise(own_key, dims, spread, limit, shards, heavy, kind=jnp.bfloat16):
    values = spread * jax.random.normal(own_key, dims, jnp.float32)
    if shards:
        values = values * block_levels(own_key, dims, shards, -0.22, 0.18)
    return jnp.clip(spiked(values, jax.random.fold_in(own_key, 3), *heavy), -limit, limit).astype(kind)


def setup_inputs(seed: int = 0, part: int = 0) -> dict:
    key_list = jax.random.split(jax.random.key(seed), 7)
    own_keys = jax.random.split(jax.random.fold_in(key_list[6], part), 7)
    tokens = draw_tokens(jax.random.fold_in(jax.random.fold_in(key_list[6], part), 71), part)
    counts = draw_counts(jax.random.fold_in(jax.random.fold_in(key_list[6], part), 71), part)
    positions = draw_positions(jax.random.fold_in(jax.random.fold_in(key_list[6], part), 71), part)
    cotangent = heavy_noise(own_keys[3], (CLIPS, FRAMES, P_SIZE, D), 1.0, 6.0, ((0, 2), (1, 4)), (0, 3, 2, 2.0))
    w_qkv = draw_w_qkv(jax.random.fold_in(key_list[6], 71), part)
    w_out = noise(key_list[5], (D, D), D ** -0.5, 0.1875, ((0, 2), (1, 2)))
    return dict(tokens=tokens, counts=counts, positions=positions, cotangent=cotangent, w_qkv=w_qkv, w_out=w_out)


epsilon = 1e-06

def narrowed(values):
    return lax.optimization_barrier(values.astype(jnp.bfloat16)).astype(jnp.float32)

def normalize(tok_grid):
    full = tok_grid.astype(jnp.float32)
    centered = full - lax.optimization_barrier(jnp.mean(full, axis=-1, keepdims=True))
    inv_std = lax.rsqrt(lax.optimization_barrier(jnp.mean(centered * centered, axis=-1, keepdims=True)) + epsilon)
    return (centered * inv_std, inv_std)

def normalize_back(d_hidden, normal, inv_std):
    centered = d_hidden - lax.optimization_barrier(jnp.mean(d_hidden, axis=-1, keepdims=True))
    return inv_std * (centered - normal * lax.optimization_barrier(jnp.mean(d_hidden * normal, axis=-1, keepdims=True)))

def attend_forward(hidden, key_mask, w_part, o_part):
    frame_count, site_count, model_width = hidden.shape
    head_count = w_part.shape[2] // HD
    scale = float(HD) ** (-0.5)
    projected = jnp.einsum('fsd,cde->cfse', hidden.astype(jnp.float32), w_part.astype(jnp.float32)).astype(jnp.bfloat16)
    shape_four = (frame_count, site_count, head_count, HD)
    queries = projected[0].reshape(shape_four)
    key_rows = projected[1].reshape(shape_four)
    value_rows = projected[2].reshape(shape_four)
    scores = jnp.einsum('fshc,gshc->shfg', queries.astype(jnp.float32), key_rows.astype(jnp.float32)) * scale
    allowed = jnp.transpose(key_mask)[:, None, None, :]
    scores = jnp.where(allowed, scores, -1e+30)
    row_top = lax.optimization_barrier(jnp.max(scores, axis=-1, keepdims=True))
    expo = jnp.exp(scores - row_top)
    attn_probs = expo / lax.optimization_barrier(jnp.sum(expo, axis=-1, keepdims=True))
    prob_bf = attn_probs.astype(jnp.bfloat16)
    attended = jnp.einsum('shfg,gshc->fshc', prob_bf.astype(jnp.float32), value_rows.astype(jnp.float32))
    attended = attended.astype(jnp.bfloat16).reshape(frame_count, site_count, head_count * HD)
    partial_out = jnp.einsum('fse,ed->fsd', attended.astype(jnp.float32), o_part.astype(jnp.float32))
    return (partial_out, (queries, key_rows, value_rows, attn_probs, prob_bf, attended))

def attend_backward(cot_grid, saved, w_part, o_part):
    queries, key_rows, value_rows, attn_probs, prob_bf, attended = saved
    frame_count, site_count, head_count, head_size = queries.shape
    scale = float(HD) ** (-0.5)
    cot_full = cot_grid.astype(jnp.float32)
    d_attended = jnp.einsum('fsd,ed->fse', cot_full, o_part.astype(jnp.float32)).astype(jnp.bfloat16)
    d_wout = jnp.einsum('fse,fsd->ed', attended.astype(jnp.float32), cot_full)
    d_heads = d_attended.reshape(queries.shape).astype(jnp.float32)
    d_probs = jnp.einsum('fshc,gshc->shfg', d_heads, value_rows.astype(jnp.float32))
    d_values = jnp.einsum('shfg,fshc->gshc', prob_bf.astype(jnp.float32), d_heads).astype(jnp.bfloat16)
    d_scores = attn_probs * (d_probs - lax.optimization_barrier(jnp.sum(d_probs * attn_probs, axis=-1, keepdims=True))) * scale
    d_scores = d_scores.astype(jnp.bfloat16).astype(jnp.float32)
    d_queries = jnp.einsum('shfg,gshc->fshc', d_scores, key_rows.astype(jnp.float32)).astype(jnp.bfloat16)
    d_keys = jnp.einsum('shfg,fshc->gshc', d_scores, queries.astype(jnp.float32)).astype(jnp.bfloat16)
    stacked = jnp.stack([d_queries, d_keys, d_values]).reshape(3, frame_count, site_count, head_count * head_size)
    d_hidden = jnp.einsum('cfse,cde->fsd', stacked.astype(jnp.float32), w_part.astype(jnp.float32))
    return (d_hidden, d_wout)

def single_clip(w_qkv, w_out, clip_args):
    tok_rows, count_row, slot_rows, cot_rows = clip_args
    slot_ids = jnp.arange(P_SIZE, dtype=jnp.int32)
    selector = (slot_rows[:, None, :] == slot_ids[None, :, None]) & (slot_ids[None, None, :] < count_row[:, None, None])
    selector = selector.astype(jnp.float32)
    tok_grid = jnp.einsum('fpk,fkd->fpd', selector, tok_rows.astype(jnp.float32)).astype(jnp.bfloat16)
    cot_grid = jnp.einsum('fpk,fkd->fpd', selector, cot_rows.astype(jnp.float32)).astype(jnp.bfloat16)
    key_mask = lax.optimization_barrier(jnp.sum(selector, axis=2)) > 0.5
    normal, inv_std = normalize(tok_grid)
    hidden = normal.astype(jnp.bfloat16)
    group_width = D // N_HEAD
    out_sum = jnp.zeros(tok_grid.shape, jnp.float32)
    saved_list = []
    for group in range(N_HEAD):
        w_part = w_qkv[:, :, group * group_width:(group + 1) * group_width]
        o_part = w_out[group * group_width:(group + 1) * group_width, :]
        partial_out, saved = attend_forward(hidden, key_mask, w_part, o_part)
        out_sum = out_sum + narrowed(partial_out)
        saved_list.append(saved)
    out_grid = (tok_grid.astype(jnp.float32) + out_sum).astype(jnp.bfloat16)
    back_sum = jnp.zeros(tok_grid.shape, jnp.float32)
    grad_parts = []
    for group in range(N_HEAD):
        w_part = w_qkv[:, :, group * group_width:(group + 1) * group_width]
        o_part = w_out[group * group_width:(group + 1) * group_width, :]
        d_part, d_wout = attend_backward(cot_grid, saved_list[group], w_part, o_part)
        back_sum = back_sum + narrowed(d_part)
        grad_parts.append(d_wout)
    grad_grid = (cot_grid.astype(jnp.float32) + normalize_back(back_sum, normal, inv_std)).astype(jnp.bfloat16)
    block_out = jnp.einsum('fpk,fpd->fkd', selector, out_grid.astype(jnp.float32)).astype(jnp.bfloat16)
    token_grad = jnp.einsum('fpk,fpd->fkd', selector, grad_grid.astype(jnp.float32)).astype(jnp.bfloat16)
    return (block_out, token_grad, jnp.concatenate(grad_parts, axis=0))

def reference(tokens, counts, positions, cotangent, w_qkv, w_out):
    results = lax.map(lambda clip_args: single_clip(w_qkv, w_out, clip_args), (tokens, counts, positions, cotangent))
    return (results[0], results[1], lax.optimization_barrier(jnp.sum(results[2], axis=0)))
```

```python
import functools

import jax
import jax.numpy as jnp
from jax import lax
from jax.experimental import pallas as pl
from jax.experimental.pallas import tpu as pltpu
from jax.sharding import PartitionSpec as P

HD = 64
PAIR = 2 * HD
EPS = 1e-06
BF = jnp.bfloat16
F32 = jnp.float32


def dot(a, b, ca, cb):
    return lax.dot_general(a, b, (((ca,), (cb,)), ((), ())), preferred_element_type=F32)


def remote(src, dst, sems, index, device):
    return pltpu.make_async_remote_copy(
        src_ref=src,
        dst_ref=dst,
        send_sem=sems[0].at[index],
        recv_sem=sems[1].at[index],
        device_id=device,
        device_id_type=pl.DeviceIdType.MESH,
    )


def kernel(
    dims, code_row, code_col, tok_ref, cot_ref, wqkv_ref, wout_ref,
    bo_ref, tg_ref, dw_ref,
    wbuf, obuf, tok_send, tok_grid, cot_send, cot_grid,
    normal_ref, inv_ref, hidden_ref, bias_ref, qkv, dqkv, att, datt, probs, wide,
    out_send, out_ret, grad_send, grad_ret,
    dw_own, dw_send, dw_recv, dwx_own, dwx_send, dwx_recv, dwz_send, dwz_recv, dwa,
    local_sem, wx0, wx1, wy0, wy1, wc0, wc1, cx0, cx1, cy0, cy1,
    zt0, zt1, zc0, zc1, zo0, zo1, zg0, zg1, ro0, ro1, rg0, rg1,
    dc0, dc1, dx0, dx1, ds0, ds1, da0, da1,
):
    T, X, G, H, FL, S, D, E, DL = dims
    rows = T * FL * S
    block = FL * S
    wx, wy, wc, cx, cy = (wx0, wx1), (wy0, wy1), (wc0, wc1), (cx0, cx1), (cy0, cy1)
    zt, zc, zo, zg = (zt0, zt1), (zc0, zc1), (zo0, zo1), (zg0, zg1)
    ro, rg, dc, dx, ds, da = (ro0, ro1), (rg0, rg1), (dc0, dc1), (dx0, dx1), (ds0, ds1), (da0, da1)
    g, z, x, h = (lax.axis_index(name) for name in ("groups", "tm", "dp", "head"))
    other_g, other_h = lax.rem(g + 1, G), lax.rem(h + 1, H)
    to_group, to_core = {"groups": other_g}, {"head": other_h}
    plus = lambda me, step, size: lax.rem(me + step, size)

    barrier = pltpu.get_barrier_semaphore()
    peers = [to_group, to_core]
    peers += [{"tm": plus(z, j, T)} for j in range(1, T)]
    peers += [{"dp": plus(x, j, X)} for j in range(1, X)]
    for peer in peers:
        pl.semaphore_signal(barrier, inc=1, device_id=peer, device_id_type=pl.DeviceIdType.MESH)
    pl.semaphore_wait(barrier, len(peers))

    pending = []

    def go(copy):
        copy.start()
        pending.append(copy)

    def w_in(i, half):
        if i < 3:
            return wqkv_ref.at[i, pl.ds(half * (DL // 2), DL // 2)]
        return wout_ref.at[pl.ds(half * (E // 2), E // 2)]

    def w_at(hh, xx, i, half):
        if i < 3:
            return wbuf.at[hh, xx, i, pl.ds(half * (DL // 2), DL // 2)]
        return obuf.at[hh, xx, pl.ds(half * (E // 2), E // 2)]

    def w_all(hh, xx, i):
        return wbuf.at[hh, xx, i] if i < 3 else obuf.at[hh, xx]

    for i in range(4):
        for j in range(1, X):
            go(remote(w_in(i, g), w_at(h, x, i, g), wx, (j - 1) * 4 + i, {"dp": plus(x, j, X)}))
    locals_ = []
    for i in range(4):
        mine = wqkv_ref.at[i] if i < 3 else wout_ref
        go(remote(mine, w_all(h, x, i), wc, i, to_core))
        copy = pltpu.make_async_copy(mine, w_all(h, x, i), local_sem.at[i])
        copy.start()
        locals_.append(copy)

    slots = code_row.shape[1]
    positions = slots // FL

    def row_code(shape, dim, core):
        r = lax.broadcasted_iota(jnp.int32, shape, dim)
        t = lax.div(r, block)
        f = lax.rem(lax.div(r, S), FL)
        s = lax.rem(r, S)
        return f * positions + (t * H + core) * S + s

    picked = row_code((rows, slots), 0, h) == code_row[...]
    chosen = jnp.where(picked, 1.0, 0.0)
    flags = jnp.sum(chosen, axis=1, keepdims=True)
    chosen = chosen.astype(BF)
    tok_send[:, :, :D] = dot(chosen, tok_ref[...], 1, 0).astype(BF).reshape(T, block, D)
    tok_send[:, :, D:] = jnp.broadcast_to(flags, (rows, 128)).astype(BF).reshape(T, block, 128)
    for j in range(1, T):
        t = plus(z, j, T)
        go(remote(tok_send.at[t], tok_grid.at[z], zt, j - 1, {"tm": t}))
    tok_grid[z] = tok_send[z]
    cot_send[...] = dot(chosen, cot_ref[...], 1, 0).astype(BF).reshape(T, block, D)
    for j in range(1, T):
        t = plus(z, j, T)
        go(remote(cot_send.at[t], cot_grid.at[z], zc, j - 1, {"tm": t}))
    cot_grid[z] = cot_send[z]

    def arrived(dst, sems, index, device):
        remote(dst, dst, sems, index, device).wait_recv()

    def forward_x(i):
        for j in range(1, X):
            src = plus(x, X - j, X)
            spot = w_at(h, src, i, g)
            arrived(spot, wx, (j - 1) * 4 + i, to_group)
            go(remote(spot, spot, wy, (j - 1) * 4 + i, to_group))
            go(remote(spot, spot, cx, (j - 1) * 4 + i, to_core))

    def forward_y(i):
        for j in range(1, X):
            src = plus(x, X - j, X)
            spot = w_at(h, src, i, other_g)
            arrived(spot, wy, (j - 1) * 4 + i, to_group)
            go(remote(spot, spot, cy, (j - 1) * 4 + i, to_core))

    def have_weights(i):
        locals_[i].wait()
        arrived(w_all(other_h, x, i), wc, i, to_core)
        for j in range(1, X):
            src = plus(x, X - j, X)
            arrived(w_at(other_h, src, i, g), cx, (j - 1) * 4 + i, to_core)
            arrived(w_at(other_h, src, i, other_g), cy, (j - 1) * 4 + i, to_core)

    forward_x(0)
    for j in range(1, T):
        arrived(tok_grid.at[plus(z, T - j, T)], zt, j - 1, to_core)

    full = tok_grid[:, :, :D].reshape(rows, D).astype(F32)
    centered = full - jnp.mean(full, axis=1, keepdims=True)
    inv_std = lax.rsqrt(jnp.mean(centered * centered, axis=1, keepdims=True) + EPS)
    normal = centered * inv_std
    normal_ref[...] = normal
    inv_ref[...] = jnp.broadcast_to(inv_std, inv_ref.shape)
    hidden_ref[...] = normal.astype(BF)
    first = jnp.where(lax.broadcasted_iota(jnp.int32, (16, 128), 1) == 0, 1.0, 0.0).astype(BF)
    keep = dot(first, tok_grid[:, :, D:].reshape(rows, 128), 1, 1)[0:1, :]
    ri = lax.broadcasted_iota(jnp.int32, (rows, rows), 0)
    ci = lax.broadcasted_iota(jnp.int32, (rows, rows), 1)
    allowed = (lax.rem(ri, S) == lax.rem(ci, S)) & (keep > 0.5)
    bias_ref[...] = jnp.where(allowed, 0.0, -1e30)

    def matmul_w(i, hh):
        total = jnp.zeros((rows, E), F32)
        for xx in range(X):
            total += dot(hidden_ref[:, xx * DL:(xx + 1) * DL], wbuf[hh, xx, i], 1, 0)
        return total.astype(BF)

    forward_x(1)
    forward_y(0)
    forward_x(2)
    have_weights(0)
    for hh in range(H):
        qkv[0, hh] = matmul_w(0, hh)
    forward_y(1)
    forward_x(3)
    have_weights(1)
    for hh in range(H):
        qkv[1, hh] = matmul_w(1, hh)
    forward_y(2)
    have_weights(2)
    for hh in range(H):
        qkv[2, hh] = matmul_w(2, hh)
    forward_y(3)

    pairs = E // PAIR
    scale = float(HD) ** (-0.5)
    lane = lax.broadcasted_iota(jnp.int32, (rows, PAIR), 1)
    left = lane < HD

    def half_of(value, second):
        keep_it = left if second == 0 else jnp.logical_not(left)
        return jnp.where(keep_it, value, jnp.zeros_like(value))

    def fwd(n, carry):
        hh, c = lax.div(n, pairs), lax.rem(n, pairs)
        cols = pl.ds(pl.multiple_of(c * PAIR, PAIR), PAIR)
        q, k, v = qkv[0, hh, :, cols], qkv[1, hh, :, cols], qkv[2, hh, :, cols]
        result = []
        for second in range(2):
            scores = dot(half_of(q, second), k, 1, 1) * scale + bias_ref[...]
            top = jnp.max(scores, axis=1, keepdims=True)
            expo = jnp.exp(scores - top)
            p = expo / jnp.sum(expo, axis=1, keepdims=True)
            probs[n, second] = p
            result.append(dot(p.astype(BF), v, 1, 0))
        att[hh, :, cols] = jnp.where(left, result[0], result[1]).astype(BF)
        return carry

    lax.fori_loop(0, H * pairs, fwd, 0)

    have_weights(3)
    for xx in range(X):
        total = jnp.zeros((rows, DL), F32)
        for hh in range(H):
            total += dot(att[hh], obuf[hh, xx], 1, 0).astype(BF).astype(F32)
        mine = tok_grid[:, :, xx * DL:(xx + 1) * DL].reshape(rows, DL).astype(F32)
        out_send[:, :, xx * DL:(xx + 1) * DL] = (mine + total).astype(BF).reshape(T, block, DL)
    for j in range(1, T):
        t = plus(z, j, T)
        go(remote(out_send.at[t], out_ret.at[h, z], zo, j - 1, {"tm": t}))
    out_ret[h, z] = out_send[z]
    go(remote(out_ret.at[h, z], out_ret.at[h, z], ro, 0, to_core))

    for j in range(1, T):
        arrived(cot_grid.at[plus(z, T - j, T)], zc, j - 1, to_core)

    def cot_cols(xx):
        return cot_grid[:, :, xx * DL:(xx + 1) * DL].reshape(rows, DL)

    for xx in range(X):
        dw_send[xx] = dot(att[other_h], cot_cols(xx), 0, 0).astype(BF)
    go(remote(dw_send, dw_recv, dc, 0, to_core))
    for xx in range(X):
        dw_own[xx] = dot(att[h], cot_cols(xx), 0, 0)

    for hh in range(H):
        total = jnp.zeros((rows, E), F32)
        for xx in range(X):
            total += dot(cot_cols(xx), obuf[hh, xx], 1, 1)
        datt[hh] = total.astype(BF)

    arrived(dw_recv, dc, 0, to_core)
    for j in range(1, X):
        to = plus(x, j, X)
        dwx_send[j - 1] = (dw_own[to] + dw_recv[to].astype(F32)).astype(BF)
        go(remote(dwx_send.at[j - 1], dwx_recv.at[j - 1], dx, j - 1, {"dp": to}))
    dwx_own[...] = dw_own[x] + dw_recv[x].astype(F32)

    def bwd(n, carry):
        hh, c = lax.div(n, pairs), lax.rem(n, pairs)
        cols = pl.ds(pl.multiple_of(c * PAIR, PAIR), PAIR)
        q, k, v = qkv[0, hh, :, cols], qkv[1, hh, :, cols], qkv[2, hh, :, cols]
        da_ = datt[hh, :, cols]
        dq, dk, dv = [], [], []
        for second in range(2):
            p = probs[n, second]
            dp_ = dot(half_of(da_, second), v, 1, 1)
            d_s = p * (dp_ - jnp.sum(dp_ * p, axis=1, keepdims=True)) * scale
            d_s = d_s.astype(BF)
            dv.append(dot(p.astype(BF), da_, 0, 0))
            dq.append(dot(d_s, k, 1, 0))
            dk.append(dot(d_s, q, 0, 0))
        dqkv[0, hh, :, cols] = jnp.where(left, dq[0], dq[1]).astype(BF)
        dqkv[1, hh, :, cols] = jnp.where(left, dk[0], dk[1]).astype(BF)
        dqkv[2, hh, :, cols] = jnp.where(left, dv[0], dv[1]).astype(BF)
        return carry

    lax.fori_loop(0, H * pairs, bwd, 0)

    for j in range(1, T):
        spot = out_ret.at[h, plus(z, T - j, T)]
        arrived(spot, zo, j - 1, to_core)
        go(remote(spot, spot, ro, j, to_core))

    for xx in range(X):
        total = jnp.zeros((rows, DL), F32)
        for hh in range(H):
            part = jnp.zeros((rows, DL), F32)
            for i in range(3):
                part += dot(dqkv[i, hh], wbuf[hh, xx, i], 1, 1)
            total += part.astype(BF).astype(F32)
        wide[:, xx * DL:(xx + 1) * DL] = total
    d_hidden = wide[...]
    normal = normal_ref[...]
    centered = d_hidden - jnp.mean(d_hidden, axis=1, keepdims=True)
    back = centered - normal * jnp.mean(d_hidden * normal, axis=1, keepdims=True)
    grad = cot_grid[...].reshape(rows, D).astype(F32) + inv_ref[:, 0:1] * back
    grad_send[...] = grad.astype(BF).reshape(T, block, D)
    for j in range(1, T):
        t = plus(z, j, T)
        go(remote(grad_send.at[t], grad_ret.at[h, z], zg, j - 1, {"tm": t}))
    grad_ret[h, z] = grad_send[z]
    go(remote(grad_ret.at[h, z], grad_ret.at[h, z], rg, 0, to_core))

    for j in range(1, X):
        arrived(dwx_recv.at[j - 1], dx, j - 1, to_core)
        dwx_own[...] += dwx_recv[j - 1].astype(F32)
    ET = E // T
    for j in range(1, T):
        t = plus(z, j, T)
        dwz_send[j - 1] = dwx_own[pl.ds(pl.multiple_of(t * ET, ET), ET), :].astype(BF)
        go(remote(dwz_send.at[j - 1], dwz_recv.at[j - 1], ds, j - 1, {"tm": t}))
    total = dwx_own[pl.ds(pl.multiple_of(z * ET, ET), ET), :]

    def back_code(shape, dim):
        r = lax.broadcasted_iota(jnp.int32, shape, dim)
        core = lax.div(r, rows)
        r = lax.rem(r, rows)
        t = lax.div(r, block)
        f = lax.rem(lax.div(r, S), FL)
        s = lax.rem(r, S)
        return f * positions + (t * H + core) * S + s

    unpick = jnp.where(code_col[...] == back_code((slots, H * rows), 1), 1.0, 0.0).astype(BF)
    for j in range(T):
        spot = out_ret.at[other_h, plus(z, T - j, T)]
        arrived(spot, ro, j, to_core)
    bo_ref[...] = dot(unpick, out_ret[...].reshape(H * rows, D), 1, 0).astype(BF)

    for j in range(1, T):
        arrived(dwz_recv.at[j - 1], ds, j - 1, to_core)
        total += dwz_recv[j - 1].astype(F32)
    dwa[z] = total.astype(BF)
    for j in range(1, T):
        go(remote(dwa.at[z], dwa.at[z], da, j - 1, {"tm": plus(z, j, T)}))

    for j in range(1, T):
        spot = grad_ret.at[h, plus(z, T - j, T)]
        arrived(spot, zg, j - 1, to_core)
        go(remote(spot, spot, rg, j, to_core))
    for j in range(T):
        arrived(grad_ret.at[other_h, plus(z, T - j, T)], rg, j, to_core)
    tg_ref[...] = dot(unpick, grad_ret[...].reshape(H * rows, D), 1, 0).astype(BF)
    for j in range(1, T):
        arrived(dwa.at[plus(z, T - j, T)], da, j - 1, to_core)
    dw_ref[...] = dwa[...].reshape(E, DL).astype(F32)
    for copy in pending:
        copy.wait_send()


def on_device(sizes, tokens, counts, positions, cotangent, w_qkv, w_out):
    G, T, X, H = sizes
    _, FL, slots, D = tokens.shape
    S = slots // (T * H)
    _, DL, E = w_qkv.shape
    rows, block = T * FL * S, FL * S
    frame = jnp.arange(FL, dtype=jnp.int32)[:, None] * slots
    kept = jnp.arange(slots, dtype=jnp.int32)[None, :] < counts[0][:, None]
    code = jnp.where(kept, positions[0] + frame, -1)
    dims = (T, X, G, H, FL, S, D, E, DL)
    pairs = E // PAIR
    vm = lambda *a: pltpu.VMEM(a[:-1], a[-1])
    sem = lambda n: [pltpu.SemaphoreType.DMA((n,))] * 2
    scratch = [
        vm(H, X, 3, DL, E, BF), vm(H, X, E, DL, BF),
        vm(T, block, D + 128, BF), vm(T, block, D + 128, BF), vm(T, block, D, BF), vm(T, block, D, BF),
        vm(rows, D, F32), vm(rows, 128, F32), vm(rows, D, BF), vm(rows, rows, F32),
        vm(3, H, rows, E, BF), vm(3, H, rows, E, BF), vm(H, rows, E, BF), vm(H, rows, E, BF),
        vm(H * pairs, 2, rows, rows, F32), vm(rows, D, F32),
        vm(T, block, D, BF), vm(H, T, block, D, BF), vm(T, block, D, BF), vm(H, T, block, D, BF),
        vm(X, E, DL, F32), vm(X, E, DL, BF), vm(X, E, DL, BF),
        vm(E, DL, F32), vm(X - 1, E, DL, BF), vm(X - 1, E, DL, BF),
        vm(T - 1, E // T, DL, BF), vm(T - 1, E // T, DL, BF), vm(T, E // T, DL, BF),
        pltpu.SemaphoreType.DMA((4,)),
    ]
    nx = 4 * (X - 1)
    for n in (nx, nx, 4, nx, nx, T - 1, T - 1, T - 1, T - 1, T, T, 1, X - 1, T - 1, T - 1):
        scratch += sem(n)
    in_vmem = pl.BlockSpec(memory_space=pltpu.VMEM)
    in_any = pl.BlockSpec(memory_space=pl.ANY)
    out, grad, dw = pl.pallas_call(
        functools.partial(kernel, dims),
        out_shape=(
            jax.ShapeDtypeStruct((FL * slots, D), BF),
            jax.ShapeDtypeStruct((FL * slots, D), BF),
            jax.ShapeDtypeStruct((E, DL), F32),
        ),
        in_specs=[in_vmem] * 4 + [in_any] * 2,
        out_specs=(in_vmem,) * 3,
        scratch_shapes=scratch,
        compiler_params=pltpu.CompilerParams(
            collective_id=0, has_side_effects=True, vmem_limit_bytes=58 * 1024 * 1024
        ),
    )(
        code.reshape(1, FL * slots), code.reshape(FL * slots, 1),
        tokens.reshape(FL * slots, D), cotangent.reshape(FL * slots, D), w_qkv, w_out,
    )
    return (out.reshape(tokens.shape), grad.reshape(tokens.shape), dw)


def solution(mesh):
    sizes = tuple(mesh.shape[name] for name in ("groups", "tm", "dp", "head"))
    placed = (
        P(("groups", "dp"), "tm", None, None),
        P(("groups", "dp"), "tm"),
        P(("groups", "dp"), "tm", None),
        P(("groups", "dp"), "tm", None, None),
        P(None, "dp", "head"),
        P("head", "dp"),
    )
    return jax.shard_map(
        functools.partial(on_device, sizes),
        mesh=mesh,
        in_specs=placed,
        out_specs=(
            P(("groups", "dp"), "tm", None, None),
            P(("groups", "dp"), "tm", None, None),
            P(("groups", "head"), "dp"),
        ),
        check_vma=False,
    )
```

```python
import functools

import jax
import jax.numpy as jnp
from jax import lax
from jax.experimental import pallas as pl
from jax.experimental.pallas import tpu as pltpu
from jax.sharding import PartitionSpec as P

HD = 64
PAIR = 2 * HD
PIECES = 2
EPS = 1e-06
BF = jnp.bfloat16
F32 = jnp.float32


def dot(a, b, ca, cb):
    return lax.dot_general(a, b, (((ca,), (cb,)), ((), ())), preferred_element_type=F32)


def remote(src, dst, sems, index, device):
    return pltpu.make_async_remote_copy(
        src_ref=src,
        dst_ref=dst,
        send_sem=sems[0].at[index],
        recv_sem=sems[1].at[index],
        device_id=device,
        device_id_type=pl.DeviceIdType.MESH,
    )


def kernel(
    dims, code_row, code_col, tok_ref, cot_ref, wqkv_ref, wout_ref,
    bo_ref, tg_ref, dw_ref,
    wbuf, obuf, tok_send, tok_grid, cot_send, cot_grid,
    normal_ref, inv_ref, hidden_ref, bias_ref, qkv, dqkv, att, datt, probs, wide,
    out_send, out_ret, grad_send, grad_ret,
    dw_own, dw_send, dw_recv, dwx_send, dwx_recv, dwz_send, dwz_recv, dwa,
    local_sem, wx0, wx1, wy0, wy1, wc0, wc1, cx0, cx1, cy0, cy1,
    zt0, zt1, zc0, zc1, zo0, zo1, zg0, zg1, ro0, ro1, rg0, rg1,
    dc0, dc1, dx0, dx1, ds0, ds1, da0, da1,
):
    T, X, G, H, FL, S, D, E, DL = dims
    rows = T * FL * S
    block = FL * S
    wx, wy, wc, cx, cy = (wx0, wx1), (wy0, wy1), (wc0, wc1), (cx0, cx1), (cy0, cy1)
    zt, zc, zo, zg = (zt0, zt1), (zc0, zc1), (zo0, zo1), (zg0, zg1)
    ro, rg, dc, dx, ds, da = (ro0, ro1), (rg0, rg1), (dc0, dc1), (dx0, dx1), (ds0, ds1), (da0, da1)
    g, z, x, h = (lax.axis_index(name) for name in ("groups", "tm", "dp", "head"))
    other_g, other_h = lax.rem(g + 1, G), lax.rem(h + 1, H)
    to_group, to_core = {"groups": other_g}, {"head": other_h}
    plus = lambda me, step, size: lax.rem(me + step, size)

    barrier = pltpu.get_barrier_semaphore()
    peers = [to_group, to_core]
    peers += [{"tm": plus(z, j, T)} for j in range(1, T)]
    peers += [{"dp": plus(x, j, X)} for j in range(1, X)]
    for peer in peers:
        pl.semaphore_signal(barrier, inc=1, device_id=peer, device_id_type=pl.DeviceIdType.MESH)
    pl.semaphore_wait(barrier, len(peers))

    pending = []

    def go(copy):
        copy.start()
        pending.append(copy)

    def unit_rows(u, half):
        size = (DL if u < 3 * PIECES else E) // (2 * PIECES)
        return pl.ds(pl.multiple_of((half * PIECES + u % PIECES) * size, size), size)

    def w_in(u, half):
        if u < 3 * PIECES:
            return wqkv_ref.at[u // PIECES, unit_rows(u, half)]
        return wout_ref.at[unit_rows(u, half)]

    def w_at(hh, xx, u, half):
        if u < 3 * PIECES:
            return wbuf.at[hh, xx, u // PIECES, unit_rows(u, half)]
        return obuf.at[hh, xx, unit_rows(u, half)]

    def w_all(hh, xx, i):
        return wbuf.at[hh, xx, i] if i < 3 else obuf.at[hh, xx]

    units = 4 * PIECES
    for u in range(units):
        for j in range(1, X):
            go(remote(w_in(u, g), w_at(h, x, u, g), wx, (j - 1) * units + u, {"dp": plus(x, j, X)}))
    locals_ = []
    for i in range(4):
        mine = wqkv_ref.at[i] if i < 3 else wout_ref
        go(remote(mine, w_all(h, x, i), wc, i, to_core))
        copy = pltpu.make_async_copy(mine, w_all(h, x, i), local_sem.at[i])
        copy.start()
        locals_.append(copy)

    slots = code_row.shape[1]
    positions = slots // FL

    def row_code(shape, dim, core):
        r = lax.broadcasted_iota(jnp.int32, shape, dim)
        t = lax.div(r, block)
        f = lax.rem(lax.div(r, S), FL)
        s = lax.rem(r, S)
        return f * positions + (t * H + core) * S + s

    picked = row_code((rows, slots), 0, h) == code_row[...]
    chosen = jnp.where(picked, 1.0, 0.0)
    flags = jnp.sum(chosen, axis=1, keepdims=True)
    chosen = chosen.astype(BF)
    tok_send[:, :, :D] = dot(chosen, tok_ref[...], 1, 0).astype(BF).reshape(T, block, D)
    tok_send[:, :, D:] = jnp.broadcast_to(flags, (rows, 128)).astype(BF).reshape(T, block, 128)
    for j in range(1, T):
        t = plus(z, j, T)
        go(remote(tok_send.at[t], tok_grid.at[z], zt, j - 1, {"tm": t}))
    tok_grid[z] = tok_send[z]
    cot_send[...] = dot(chosen, cot_ref[...], 1, 0).astype(BF).reshape(T, block, D)
    for j in range(1, T):
        t = plus(z, j, T)
        go(remote(cot_send.at[t], cot_grid.at[z], zc, j - 1, {"tm": t}))
    cot_grid[z] = cot_send[z]

    def arrived(dst, sems, index, device):
        remote(dst, dst, sems, index, device).wait_recv()

    def forward_x(u):
        for j in range(1, X):
            src = plus(x, X - j, X)
            spot = w_at(h, src, u, g)
            arrived(spot, wx, (j - 1) * units + u, to_group)
            go(remote(spot, spot, wy, (j - 1) * units + u, to_group))
            go(remote(spot, spot, cx, (j - 1) * units + u, to_core))

    def forward_y(u):
        for j in range(1, X):
            src = plus(x, X - j, X)
            spot = w_at(h, src, u, other_g)
            arrived(spot, wy, (j - 1) * units + u, to_group)
            go(remote(spot, spot, cy, (j - 1) * units + u, to_core))

    def have_weights(i):
        locals_[i].wait()
        arrived(w_all(other_h, x, i), wc, i, to_core)
        for u in range(i * PIECES, (i + 1) * PIECES):
            for j in range(1, X):
                src = plus(x, X - j, X)
                arrived(w_at(other_h, src, u, g), cx, (j - 1) * units + u, to_core)
                arrived(w_at(other_h, src, u, other_g), cy, (j - 1) * units + u, to_core)

    forward_x(0)
    for j in range(1, T):
        arrived(tok_grid.at[plus(z, T - j, T)], zt, j - 1, to_core)

    full = tok_grid[:, :, :D].reshape(rows, D).astype(F32)
    centered = full - jnp.mean(full, axis=1, keepdims=True)
    inv_std = lax.rsqrt(jnp.mean(centered * centered, axis=1, keepdims=True) + EPS)
    normal = centered * inv_std
    normal_ref[...] = normal
    inv_ref[...] = jnp.broadcast_to(inv_std, inv_ref.shape)
    hidden_ref[...] = normal.astype(BF)
    first = jnp.where(lax.broadcasted_iota(jnp.int32, (16, 128), 1) == 0, 1.0, 0.0).astype(BF)
    keep = dot(first, tok_grid[:, :, D:].reshape(rows, 128), 1, 1)[0:1, :]
    ri = lax.broadcasted_iota(jnp.int32, (rows, rows), 0)
    ci = lax.broadcasted_iota(jnp.int32, (rows, rows), 1)
    allowed = (lax.rem(ri, S) == lax.rem(ci, S)) & (keep > 0.5)
    bias_ref[...] = jnp.where(allowed, 0.0, -1e30)

    def matmul_w(i, hh):
        total = jnp.zeros((rows, E), F32)
        for xx in range(X):
            total += dot(hidden_ref[:, xx * DL:(xx + 1) * DL], wbuf[hh, xx, i], 1, 0)
        return total.astype(BF)

    def project(i):
        have_weights(i)
        for hh in range(H):
            qkv[i, hh] = matmul_w(i, hh)

    for u in range(1, units):
        forward_x(u)
        forward_y(u - 1)
        if u % PIECES == PIECES - 1 and u >= 2 * PIECES - 1:
            project(u // PIECES - 1)

    pairs = E // PAIR
    scale = float(HD) ** (-0.5)
    lane = lax.broadcasted_iota(jnp.int32, (rows, PAIR), 1)
    left = lane < HD

    def half_of(value, second):
        keep_it = left if second == 0 else jnp.logical_not(left)
        return jnp.where(keep_it, value, jnp.zeros_like(value))

    def fwd(n, carry):
        hh, c = lax.div(n, pairs), lax.rem(n, pairs)
        cols = pl.ds(pl.multiple_of(c * PAIR, PAIR), PAIR)
        q, k, v = qkv[0, hh, :, cols], qkv[1, hh, :, cols], qkv[2, hh, :, cols]
        result = []
        for second in range(2):
            scores = dot(half_of(q, second), k, 1, 1) * scale + bias_ref[...]
            top = jnp.max(scores, axis=1, keepdims=True)
            expo = jnp.exp(scores - top)
            p = expo / jnp.sum(expo, axis=1, keepdims=True)
            probs[n, second] = p
            result.append(dot(p.astype(BF), v, 1, 0))
        att[hh, :, cols] = jnp.where(left, result[0], result[1]).astype(BF)
        return carry

    lax.fori_loop(0, 2, fwd, 0)
    forward_y(units - 1)
    lax.fori_loop(2, H * pairs, fwd, 0)

    for j in range(1, T):
        arrived(cot_grid.at[plus(z, T - j, T)], zc, j - 1, to_core)

    def cot_cols(xx):
        return cot_grid[:, :, xx * DL:(xx + 1) * DL].reshape(rows, DL)

    for xx in range(X):
        dw_send[xx] = dot(att[other_h], cot_cols(xx), 0, 0).astype(BF)
    go(remote(dw_send, dw_recv, dc, 0, to_core))
    for xx in range(X):
        dw_own[xx] = dot(att[h], cot_cols(xx), 0, 0)

    have_weights(3)
    for xx in range(X):
        total = jnp.zeros((rows, DL), F32)
        for hh in range(H):
            total += dot(att[hh], obuf[hh, xx], 1, 0).astype(BF).astype(F32)
        mine = tok_grid[:, :, xx * DL:(xx + 1) * DL].reshape(rows, DL).astype(F32)
        out_send[:, :, xx * DL:(xx + 1) * DL] = (mine + total).astype(BF).reshape(T, block, DL)
    for j in range(1, T):
        t = plus(z, j, T)
        go(remote(out_send.at[t], out_ret.at[h, z], zo, j - 1, {"tm": t}))
    out_ret[h, z] = out_send[z]
    go(remote(out_ret.at[h, z], out_ret.at[h, z], ro, 0, to_core))

    for hh in range(H):
        total = jnp.zeros((rows, E), F32)
        for xx in range(X):
            total += dot(cot_cols(xx), obuf[hh, xx], 1, 1)
        datt[hh] = total.astype(BF)

    ET = E // T

    def chunk(t):
        return pl.ds(pl.multiple_of(t * ET, ET), ET)

    arrived(dw_recv, dc, 0, to_core)
    for k in range(1, T + 1):
        c = plus(z, k, T)
        for j in range(1, X):
            to = plus(x, j, X)
            both = dw_own[to, chunk(c), :] + dw_recv[to, chunk(c), :].astype(F32)
            dwx_send[j - 1, c] = both.astype(BF)
            go(remote(dwx_send.at[j - 1, c], dwx_recv.at[j - 1, c], dx, (j - 1) * T + k - 1, {"dp": to}))

    def dp_sum(k):
        c = plus(z, k, T)
        total = dw_own[x, chunk(c), :] + dw_recv[x, chunk(c), :].astype(F32)
        for j in range(1, X):
            arrived(dwx_recv.at[j - 1, c], dx, (j - 1) * T + k - 1, to_core)
            total += dwx_recv[j - 1, c].astype(F32)
        return total

    def send_chunk(k):
        dwz_send[k - 1] = dp_sum(k).astype(BF)
        go(remote(dwz_send.at[k - 1], dwz_recv.at[k - 1], ds, k - 1, {"tm": plus(z, k, T)}))

    def bwd(n, carry):
        hh, c = lax.div(n, pairs), lax.rem(n, pairs)
        cols = pl.ds(pl.multiple_of(c * PAIR, PAIR), PAIR)
        q, k, v = qkv[0, hh, :, cols], qkv[1, hh, :, cols], qkv[2, hh, :, cols]
        da_ = datt[hh, :, cols]
        dq, dk, dv = [], [], []
        for second in range(2):
            p = probs[n, second]
            dp_ = dot(half_of(da_, second), v, 1, 1)
            d_s = p * (dp_ - jnp.sum(dp_ * p, axis=1, keepdims=True)) * scale
            d_s = d_s.astype(BF)
            dv.append(dot(p.astype(BF), da_, 0, 0))
            dq.append(dot(d_s, k, 1, 0))
            dk.append(dot(d_s, q, 0, 0))
        dqkv[0, hh, :, cols] = jnp.where(left, dq[0], dq[1]).astype(BF)
        dqkv[1, hh, :, cols] = jnp.where(left, dk[0], dk[1]).astype(BF)
        dqkv[2, hh, :, cols] = jnp.where(left, dv[0], dv[1]).astype(BF)
        return carry

    parts = 4
    for part in range(parts):
        lax.fori_loop(part * H * pairs // parts, (part + 1) * H * pairs // parts, bwd, 0)
        for k in range(part * (T - 1) // parts, (part + 1) * (T - 1) // parts):
            send_chunk(k + 1)

    for j in range(1, T):
        spot = out_ret.at[h, plus(z, T - j, T)]
        arrived(spot, zo, j - 1, to_core)
        go(remote(spot, spot, ro, j, to_core))

    for xx in range(X):
        total = jnp.zeros((rows, DL), F32)
        for hh in range(H):
            part = jnp.zeros((rows, DL), F32)
            for i in range(3):
                part += dot(dqkv[i, hh], wbuf[hh, xx, i], 1, 1)
            total += part.astype(BF).astype(F32)
        wide[:, xx * DL:(xx + 1) * DL] = total
    d_hidden = wide[...]
    normal = normal_ref[...]
    centered = d_hidden - jnp.mean(d_hidden, axis=1, keepdims=True)
    back = centered - normal * jnp.mean(d_hidden * normal, axis=1, keepdims=True)
    grad = cot_grid[...].reshape(rows, D).astype(F32) + inv_ref[:, 0:1] * back
    grad_send[...] = grad.astype(BF).reshape(T, block, D)
    for j in range(1, T):
        t = plus(z, j, T)
        go(remote(grad_send.at[t], grad_ret.at[h, z], zg, j - 1, {"tm": t}))
    grad_ret[h, z] = grad_send[z]
    go(remote(grad_ret.at[h, z], grad_ret.at[h, z], rg, 0, to_core))

    total = dp_sum(T)
    for j in range(1, T):
        arrived(dwz_recv.at[j - 1], ds, j - 1, to_core)
        total += dwz_recv[j - 1].astype(F32)
    dwa[z] = total.astype(BF)
    for j in range(1, T):
        go(remote(dwa.at[z], dwa.at[z], da, j - 1, {"tm": plus(z, j, T)}))

    def back_code(shape, dim):
        r = lax.broadcasted_iota(jnp.int32, shape, dim)
        core = lax.div(r, rows)
        r = lax.rem(r, rows)
        t = lax.div(r, block)
        f = lax.rem(lax.div(r, S), FL)
        s = lax.rem(r, S)
        return f * positions + (t * H + core) * S + s

    unpick = jnp.where(code_col[...] == back_code((slots, H * rows), 1), 1.0, 0.0).astype(BF)
    for j in range(T):
        spot = out_ret.at[other_h, plus(z, T - j, T)]
        arrived(spot, ro, j, to_core)
    bo_ref[...] = dot(unpick, out_ret[...].reshape(H * rows, D), 1, 0).astype(BF)

    for j in range(1, T):
        spot = grad_ret.at[h, plus(z, T - j, T)]
        arrived(spot, zg, j - 1, to_core)
        go(remote(spot, spot, rg, j, to_core))
    for j in range(T):
        arrived(grad_ret.at[other_h, plus(z, T - j, T)], rg, j, to_core)
    tg_ref[...] = dot(unpick, grad_ret[...].reshape(H * rows, D), 1, 0).astype(BF)
    for j in range(1, T):
        arrived(dwa.at[plus(z, T - j, T)], da, j - 1, to_core)
    dw_ref[...] = dwa[...].reshape(E, DL)
    for copy in pending:
        copy.wait_send()


def on_device(sizes, tokens, counts, positions, cotangent, w_qkv, w_out):
    G, T, X, H = sizes
    _, FL, slots, D = tokens.shape
    S = slots // (T * H)
    _, DL, E = w_qkv.shape
    rows, block = T * FL * S, FL * S
    frame = jnp.arange(FL, dtype=jnp.int32)[:, None] * slots
    kept = jnp.arange(slots, dtype=jnp.int32)[None, :] < counts[0][:, None]
    code = jnp.where(kept, positions[0] + frame, -1)
    dims = (T, X, G, H, FL, S, D, E, DL)
    pairs = E // PAIR
    vm = lambda *a: pltpu.VMEM(a[:-1], a[-1])
    sem = lambda n: [pltpu.SemaphoreType.DMA((n,))] * 2
    scratch = [
        vm(H, X, 3, DL, E, BF), vm(H, X, E, DL, BF),
        vm(T, block, D + 128, BF), vm(T, block, D + 128, BF), vm(T, block, D, BF), vm(T, block, D, BF),
        vm(rows, D, F32), vm(rows, 128, F32), vm(rows, D, BF), vm(rows, rows, F32),
        vm(3, H, rows, E, BF), vm(3, H, rows, E, BF), vm(H, rows, E, BF), vm(H, rows, E, BF),
        vm(H * pairs, 2, rows, rows, F32), vm(rows, D, F32),
        vm(T, block, D, BF), vm(H, T, block, D, BF), vm(T, block, D, BF), vm(H, T, block, D, BF),
        vm(X, E, DL, F32), vm(X, E, DL, BF), vm(X, E, DL, BF),
        vm(X - 1, T, E // T, DL, BF), vm(X - 1, T, E // T, DL, BF),
        vm(T - 1, E // T, DL, BF), vm(T - 1, E // T, DL, BF), vm(T, E // T, DL, BF),
        pltpu.SemaphoreType.DMA((4,)),
    ]
    nx = 4 * PIECES * (X - 1)
    for n in (nx, nx, 4, nx, nx, T - 1, T - 1, T - 1, T - 1, T, T, 1, (X - 1) * T, T - 1, T - 1):
        scratch += sem(n)
    in_vmem = pl.BlockSpec(memory_space=pltpu.VMEM)
    in_any = pl.BlockSpec(memory_space=pl.ANY)
    out, grad, dw = pl.pallas_call(
        functools.partial(kernel, dims),
        out_shape=(
            jax.ShapeDtypeStruct((FL * slots, D), BF),
            jax.ShapeDtypeStruct((FL * slots, D), BF),
            jax.ShapeDtypeStruct((E, DL), BF),
        ),
        in_specs=[in_vmem] * 4 + [in_any] * 2,
        out_specs=(in_vmem,) * 3,
        scratch_shapes=scratch,
        compiler_params=pltpu.CompilerParams(
            collective_id=0, has_side_effects=True, vmem_limit_bytes=58 * 1024 * 1024
        ),
    )(
        code.reshape(1, FL * slots), code.reshape(FL * slots, 1),
        tokens.reshape(FL * slots, D), cotangent.reshape(FL * slots, D), w_qkv, w_out,
    )
    return (out.reshape(tokens.shape), grad.reshape(tokens.shape), dw.astype(F32))


def solution(mesh):
    sizes = tuple(mesh.shape[name] for name in ("groups", "tm", "dp", "head"))
    placed = (
        P(("groups", "dp"), "tm", None, None),
        P(("groups", "dp"), "tm"),
        P(("groups", "dp"), "tm", None),
        P(("groups", "dp"), "tm", None, None),
        P(None, "dp", "head"),
        P("head", "dp"),
    )
    return jax.shard_map(
        functools.partial(on_device, sizes),
        mesh=mesh,
        in_specs=placed,
        out_specs=(
            P(("groups", "dp"), "tm", None, None),
            P(("groups", "dp"), "tm", None, None),
            P(("groups", "head"), "dp"),
        ),
        check_vma=False,
    )
```
